32 devices in a mesh: dp: 4 (over y, x), expert: 8 (over z, core).
Axes of the slice: x: 2, y: 2, z: 4, core: 2. Of those that a mesh axis runs over, the one named last changes fastest.
Arguments:
- hidden: bfloat16 [4096, 2, 1024], P(('dp', 'expert')), may hold values from -6 to 6
- routes: int32 [4096, 2], P(('dp', 'expert')), may hold values from 0 to 7, all different within a row; in each aligned block of 128 rows (0 to 127, 128 to 255, ...) at most 64 rows name the same one
- gates: float32 [4096, 2], P(('dp', 'expert')), may hold values from 0.1 to 1
- cotangent: bfloat16 [4096, 7168], P(('dp', 'expert')), may hold values from -1.796875 to 1.796875
- weight: bfloat16 [8, 1024, 7168], P('expert', None, 'dp'), may hold values from -0.0625 to 0.0625
Outputs:
- grad_hidden: bfloat16 [4096, 2, 1024], P(('dp', 'expert'))
- grad_gates: float32 [4096, 2], P(('dp', 'expert'))
- grad_weight: bfloat16 [8, 1024, 7168], P('expert', None, 'dp')
The draws below stay inside these ranges and needn't reach their ends.
Inputs may be any that keep to these rules, and one draw needn't show every extreme that they name: `routes`: each row names 2 different experts; in each aligned block of 128 rows (the rows of one device) no expert is named by more than 64 rows, a bound that some block reaches.
All inputs are finite; a program needn't handle non-finite values.
Results may differ from the reference program's by a relative error of at most 0.0049.
Values may be sent and summed in bfloat16 or wider, within the bound.
A program may use at most 128 MiB of HBM per device.

```python
import math
import jax
import jax.numpy as jnp
import numpy as np
from jax import lax

D = 7168
FF = 1024
TOP = 2
TOK_DEV = 128
EXPERTS = 8
MOST = 64
TOKENS = 4096
N_DP = 4
N_EXPERT = 8


def level_of(own_key, shape, shards, least, high):
    loudness, own = 1.0, jax.random.fold_in(own_key, 6)
    for position, shards_of in shards:
        draws = jnp.exp(jax.random.uniform(jax.random.fold_in(own, position), (shards_of,), jnp.float32, least / len(shards), high / len(shards)))
        loudness = loudness * jnp.repeat(draws, shape[position] // shards_of).reshape([-1 if axis == position else 1 for axis in range(len(shape))])
    return loudness


def routed_block(rng, own, number, rows, amount, top, most, lean):
    order = jax.random.permutation(rng, amount)
    heavy_load, usual = portions_of(amount, rows * top, most, lean, True), portions_of(amount, rows * top, most, lean, False)
    places = jnp.arange(amount)

    def named(tallies, turn):
        used = int((tallies > 0).sum())
        fixed = max(1, used // 4)
        shifted = fixed + (places - fixed + turn * (used - fixed)) % max(1, amount - fixed)
        return jnp.zeros((amount,), jnp.int32).at[order[jnp.where(places < fixed, places, shifted)]].set(jnp.asarray(tallies, jnp.int32))

    tallies = jnp.where(number % 4 == 0, named(heavy_load, number // 4), named(usual, number - number // 4 - 1))
    mixed = jax.random.permutation(jax.random.fold_in(own, 3), amount)
    source_of, sink = mixed[0:amount // 2 * 2:2], mixed[1:amount // 2 * 2:2]
    room = jnp.minimum(tallies[source_of] - 1, most - tallies[sink]) // 2
    room = jnp.where((source_of == order[0]) | (sink == order[0]) | (tallies[sink] == 0), 0, jnp.maximum(room, 0))
    shifted = jax.random.randint(jax.random.fold_in(own, 4), (amount // 2,), 0, 1 << 20) % (room + 1)
    tallies = tallies.at[source_of].add(-shifted).at[sink].add(shifted)
    items = jnp.searchsorted(jnp.cumsum(tallies), jnp.arange(rows * top), side="right").astype(jnp.int32)
    listing = items.reshape(top, rows).T
    listing = listing[jax.random.permutation(jax.random.fold_in(own, 1), rows)]
    turn = jax.random.randint(jax.random.fold_in(own, 2), (rows, 1), 0, top)
    return jnp.take_along_axis(listing, (jnp.arange(top)[None, :] + turn) % top, axis=1)


def portions_of(amount, total, most, lean, full):
    weights = [(1 << 20) // math.isqrt(grade ** lean) + 1 for grade in range(1, amount + 1)]
    largest = most if full else min(most, max(-(-total // amount), total * weights[0] // sum(weights)))
    least = 1 if total - largest >= amount - 1 else 0
    counts, spare = [largest] + [least] * (amount - 1), total - largest - least * (amount - 1)
    while spare > 0:
        candidates = [i for i in range(1, amount) if counts[i] < largest] or [i for i in range(1, amount) if counts[i] < most]
        whole, remaining = sum([weights[i] for i in candidates]), spare
        for i in candidates:
            addition = min(most - counts[i], max(1, remaining * weights[i] // whole), spare)
            counts[i] = counts[i] + addition
            spare = spare - addition
    return np.array(counts)


def centred(own_key, extent, scale, reach, split=(), kind=jnp.bfloat16):
    gain = level_of(own_key, extent, split, -0.22, 0.18) if split else 1.0
    result = jax.random.normal(own_key, extent, jnp.float32) * scale * gain
    return jnp.minimum(jnp.maximum(result, -reach), reach).astype(kind)


def setup_inputs(seed: int = 0) -> dict:
    arg_keys = jax.random.split(jax.random.key(seed), 6)
    hidden = centred(arg_keys[0], (TOKENS, TOP, FF), 1.0, 6.0, ((0, 32),))
    routes_keys = jax.random.split(jax.random.fold_in(arg_keys[1], 1), TOKENS // TOK_DEV)
    routes_turns = jax.random.permutation(jax.random.fold_in(arg_keys[1], 3), TOKENS // TOK_DEV)
    routes = jax.vmap(lambda own, number: routed_block(jax.random.fold_in(arg_keys[1], 2), own, number, TOK_DEV, EXPERTS, TOP, MOST, 2))(routes_keys, routes_turns).reshape((TOKENS, TOP))
    gates = jnp.clip(jnp.exp(math.log(1.0) - 2.3025851 * jax.random.uniform(arg_keys[2], (TOKENS, TOP), jnp.float32) ** level_of(arg_keys[2], (TOKENS, TOP), ((0, 32),), -0.2, 0.2)), 0.1, 1.0)
    cotangent = centred(arg_keys[3], (TOKENS, D), 0.3, 1.796875, ((0, 32),))
    weight = centred(arg_keys[4], (EXPERTS, FF, D), D ** -0.5, 0.0625, ((0, 8), (2, 4)))
    return dict(hidden=hidden, routes=routes, gates=gates, cotangent=cotangent, weight=weight)


def reference(hidden, routes, gates, cotangent, weight):
    slot_count = TOKENS * TOP
    flat_experts = routes.reshape(slot_count).astype(jnp.int32)
    order_slots = jnp.argsort(flat_experts, stable=True).astype(jnp.int32)
    labels = jnp.arange(EXPERTS, dtype=jnp.int32)
    totals = jnp.sum((flat_experts[:, None] == labels[None, :]).astype(jnp.int32), axis=0).astype(jnp.int32)
    starts = (jnp.cumsum(totals) - totals).astype(jnp.int32)
    limit = N_DP * N_EXPERT * MOST
    padded_order = jnp.concatenate([order_slots, jnp.full((limit,), slot_count, jnp.int32)])
    scaled = (gates[:, :, None] * hidden.astype(jnp.float32)).astype(jnp.bfloat16).reshape(slot_count, FF)
    scaled_pad = jnp.concatenate([scaled, jnp.zeros((1, FF), jnp.bfloat16)], axis=0)
    cot_pad = jnp.concatenate([cotangent, jnp.zeros((1, D), jnp.bfloat16)], axis=0)

    def per_expert(expert_id):
        picked = lax.dynamic_slice_in_dim(padded_order, starts[expert_id], limit)
        valid = jnp.arange(limit, dtype=jnp.int32) < totals[expert_id]
        picked = jnp.where(valid, picked, slot_count).astype(jnp.int32)
        rows_cot = cot_pad[picked // TOP].astype(jnp.float32)
        matrix = weight[expert_id].astype(jnp.float32)
        back_rows = jnp.dot(rows_cot, matrix.T, precision=lax.Precision.HIGHEST)
        rows_scaled = scaled_pad[picked].astype(jnp.float32)
        grad_matrix = jnp.dot(rows_scaled.T, rows_cot, precision=lax.Precision.HIGHEST)
        return back_rows, grad_matrix.astype(jnp.bfloat16), picked

    back_rows, grad_weight, picked = lax.map(per_expert, labels)
    back_all = jnp.zeros((slot_count + 1, FF), jnp.float32).at[picked.reshape(-1)].set(back_rows.reshape(-1, FF))
    back = back_all[:slot_count]
    grad_hidden = (gates.reshape(slot_count)[:, None] * back).astype(jnp.bfloat16).reshape(TOKENS, TOP, FF)
    grad_gates = jnp.sum(hidden.reshape(slot_count, FF).astype(jnp.float32) * back, axis=1).reshape(TOKENS, TOP)
    return grad_hidden, grad_gates, grad_weight
```

```python
import jax
import jax.numpy as jnp
from jax import lax
from jax.sharding import PartitionSpec as P


def slots_of(routes, columns, capacity):
    tokens, top = routes.shape
    flat = routes.reshape(tokens * top)
    one_hot = (flat[:, None] == jnp.arange(columns, dtype=jnp.int32)[None, :]).astype(jnp.int32)
    earlier = jnp.cumsum(one_hot, axis=0) - one_hot
    position = jnp.sum(earlier * one_hot, axis=1)
    return flat * capacity + position


def gathered(hidden, routes, gates, cotangent, weight):
    tokens, top, width = hidden.shape
    columns, groups = lax.axis_size("expert"), lax.axis_size("dp")
    capacity = min(tokens, 2 * tokens * top // columns)
    slots = tokens * top
    part = cotangent.shape[1] // groups
    quarters = cotangent.reshape(tokens, groups, part).transpose(1, 0, 2)
    quarters = lax.all_to_all(quarters, "dp", split_axis=0, concat_axis=0, tiled=True)
    every = lax.all_gather(quarters, "expert", axis=0, tiled=False)

    destination = slots_of(routes, columns, capacity)
    slot_of = (
        jnp.full((columns * capacity,), slots, jnp.int32)
        .at[destination]
        .set(jnp.arange(slots, dtype=jnp.int32))
    )
    scaled = (
        (gates[:, :, None] * hidden.astype(jnp.float32)).astype(jnp.bfloat16).reshape(slots, width)
    )
    scaled = jnp.concatenate([scaled, jnp.zeros((1, width), jnp.bfloat16)], axis=0)
    rows = scaled[slot_of].reshape(columns, capacity, width)
    token_of = (slot_of // top).reshape(columns, capacity)
    rows = lax.all_to_all(rows, "expert", split_axis=0, concat_axis=0, tiled=True)
    token_of = lax.all_to_all(token_of, "expert", split_axis=0, concat_axis=0, tiled=True)
    rows = lax.all_gather(rows, "dp", axis=0, tiled=False)
    token_of = lax.all_gather(token_of, "dp", axis=0, tiled=False)

    block = jnp.arange(columns)[None, :, None] * groups + jnp.arange(groups)[:, None, None]
    picked = block * tokens + jnp.minimum(token_of, tokens - 1)
    cot = every.reshape(columns * groups * tokens, part)[picked.reshape(-1)]
    matrix = weight[0]
    partial_back = lax.dot_general(
        cot, matrix, (((1,), (1,)), ((), ())), preferred_element_type=jnp.float32
    ).astype(jnp.bfloat16)
    partial_back = partial_back.reshape(groups, columns, capacity, width)
    summed = lax.psum_scatter(partial_back, "dp", scatter_dimension=0, tiled=True)
    grad_matrix = lax.dot_general(
        rows.reshape(-1, width), cot, (((0,), (0,)), ((), ())), preferred_element_type=jnp.float32
    )
    returned = lax.all_to_all(summed[0], "expert", split_axis=0, concat_axis=0, tiled=True)
    back = returned.reshape(columns * capacity, width)[destination].astype(jnp.float32)
    grad_hidden = (
        (gates.reshape(slots)[:, None] * back).astype(jnp.bfloat16).reshape(tokens, top, width)
    )
    grad_gates = jnp.sum(
        hidden.reshape(slots, width).astype(jnp.float32) * back, axis=1
    ).reshape(tokens, top)
    return (grad_hidden, grad_gates, grad_matrix.astype(jnp.bfloat16)[None])


def dispatched(hidden, routes, gates, cotangent, weight):
    local_tokens, top_count, hidden_width = hidden.shape
    columns = lax.axis_size("expert")
    capacity = min(local_tokens, 2 * local_tokens * top_count // columns)
    slot_count = local_tokens * top_count
    flat_experts = routes.reshape(slot_count)
    one_hot = (flat_experts[:, None] == jnp.arange(columns, dtype=jnp.int32)[None, :]).astype(
        jnp.int32
    )
    earlier = jnp.cumsum(one_hot, axis=0) - one_hot
    position = jnp.sum(earlier * one_hot, axis=1)
    destination = flat_experts * capacity + position
    slot_of = (
        jnp.full((columns * capacity,), slot_count, jnp.int32)
        .at[destination]
        .set(jnp.arange(slot_count, dtype=jnp.int32))
    )
    scaled = (
        (gates[:, :, None] * hidden.astype(jnp.float32))
        .astype(jnp.bfloat16)
        .reshape(slot_count, hidden_width)
    )
    scaled = jnp.concatenate([scaled, jnp.zeros((1, hidden_width), jnp.bfloat16)], axis=0)
    cot_pad = jnp.concatenate([cotangent, jnp.zeros((1, cotangent.shape[1]), jnp.bfloat16)], axis=0)
    send_rows = scaled[slot_of].reshape(columns, capacity, hidden_width)
    send_cot = cot_pad[slot_of // top_count].reshape(columns, capacity, cotangent.shape[1])
    got_rows, got_cot = (
        lax.all_to_all(send_rows, "expert", split_axis=0, concat_axis=0, tiled=True),
        lax.all_to_all(send_cot, "expert", split_axis=0, concat_axis=0, tiled=True),
    )
    cot_quarter = lax.all_to_all(got_cot[None], "dp", split_axis=3, concat_axis=0, tiled=True)
    rows_all = lax.all_gather(got_rows[None], "dp", axis=0, tiled=True)
    matrix = weight[0]
    partial_back = jnp.einsum(
        "bscd,fd->bscf", cot_quarter, matrix, preferred_element_type=jnp.float32
    )
    summed = lax.psum_scatter(partial_back, "dp", scatter_dimension=0, tiled=True)
    grad_matrix = jnp.einsum(
        "bscf,bscd->fd", rows_all, cot_quarter, preferred_element_type=jnp.float32
    )
    returned = lax.all_to_all(summed[0], "expert", split_axis=0, concat_axis=0, tiled=True)
    back = returned.reshape(columns * capacity, hidden_width)[destination]
    grad_hidden = (
        (gates.reshape(slot_count)[:, None] * back)
        .astype(jnp.bfloat16)
        .reshape(local_tokens, top_count, hidden_width)
    )
    grad_gates = jnp.sum(
        hidden.reshape(slot_count, hidden_width).astype(jnp.float32) * back, axis=1
    ).reshape(local_tokens, top_count)
    return (grad_hidden, grad_gates, grad_matrix.astype(jnp.bfloat16)[None])


def per_device(hidden, routes, gates, cotangent, weight):
    tokens, top = routes.shape
    capacity = min(tokens, 2 * tokens * top // lax.axis_size("expert"))
    form = gathered if tokens <= 2 * capacity else dispatched
    return form(hidden, routes, gates, cotangent, weight)


def solution(mesh):
    placed = (
        P(("dp", "expert"), None, None),
        P(("dp", "expert"), None),
        P(("dp", "expert"), None),
        P(("dp", "expert"), None),
        P("expert", None, "dp"),
    )
    return jax.shard_map(
        per_device,
        mesh=mesh,
        in_specs=placed,
        out_specs=(
            P(("dp", "expert"), None, None),
            P(("dp", "expert"), None),
            P("expert", None, "dp"),
        ),
        check_vma=False,
    )
```

```python
import functools

import jax
import jax.numpy as jnp
from jax import lax
from jax.experimental import pallas as pl
from jax.experimental.pallas import tpu as pltpu
from jax.sharding import PartitionSpec as P

MESH = pl.DeviceIdType.MESH


def exchange(groups, columns, quarters, packed, every, rows, local_sem, dp_send, dp_recv, side_send,
             up_send, down_send, line_recv, side_recv, rows_send, rows_recv, pass_send, pass_recv):
    group, mine = lax.axis_index("dp"), lax.axis_index("expert")
    depth = columns // 2
    level, core = mine // 2, lax.rem(mine, 2)

    def other(index, step, size):
        return lax.rem(index + step, size)

    barrier = pltpu.get_barrier_semaphore()
    for step in range(1, groups):
        pl.semaphore_signal(barrier, inc=1, device_id=(other(group, step, groups), mine), device_id_type=MESH)
    for step in range(1, columns):
        pl.semaphore_signal(barrier, inc=1, device_id=(group, other(mine, step, columns)), device_id_type=MESH)
    pl.semaphore_wait(barrier, groups + columns - 2)

    def remote(source, target, send, recv, device):
        return pltpu.make_async_remote_copy(
            src_ref=source, dst_ref=target, send_sem=send, recv_sem=recv, device_id=device, device_id_type=MESH
        )

    def to_group(step):
        there = other(group, step, groups)
        return remote(quarters.at[there], every.at[group, mine], dp_send.at[step], dp_recv.at[step], (there, mine))

    def to_expert(step):
        there = other(mine, step, columns)
        return remote(packed.at[there], rows.at[group, mine], rows_send.at[step], rows_recv.at[step], (group, there))

    def chunk(start, step):
        source = lax.rem(group - step + groups, groups)
        place = every.at[source, start * 2 + core]
        return place, source

    def on_line(start, step, move, first=False):
        place, source = chunk(start, step)
        send = (up_send if move > 0 else down_send).at[start, step]
        origin = quarters.at[group] if first else place
        return remote(origin, place, send, line_recv.at[start, step], (group, (level + move) * 2 + core))

    def to_side(start, step, first=False):
        place, source = chunk(start, step)
        origin = quarters.at[group] if first else place
        return remote(origin, place, side_send.at[start, step], side_recv.at[start, step], (group, level * 2 + 1 - core))

    def pass_on(step, hop):
        start = lax.rem(mine - step + columns, columns)
        place = rows.at[group, start]
        origin = packed.at[mine] if step == 0 else place
        return remote(origin, place, pass_send.at[hop, step], pass_recv.at[hop, step], (other(group, hop, groups), mine))

    own_cot = pltpu.make_async_copy(quarters.at[group], every.at[group, mine], local_sem.at[0])
    own_rows = pltpu.make_async_copy(packed.at[mine], rows.at[group, mine], local_sem.at[1])

    for step in range(1, groups):
        to_group(step).start()
    for step in range(groups):
        if step:
            to_group(step).wait_recv()
        first = step == 0

        @pl.when(level < depth - 1)
        def _():
            on_line(level, step, 1, first).start()

        @pl.when(level > 0)
        def _():
            on_line(level, step, -1, first).start()

        to_side(level, step, first).start()
        if first:
            own_cot.start()
            own_rows.start()
            for peer in range(1, columns):
                to_expert(peer).start()
            for hop in range(1, groups):
                pass_on(0, hop).start()
    for distance in range(1, depth):
        for step in range(groups):
            for move in (1, -1):
                start = level - move * distance
                inside = (start >= 0) & (start < depth)
                onward = (level < depth - 1) if move > 0 else (level > 0)

                @pl.when(inside)
                def _():
                    on_line(start, step, move).wait_recv()
                    to_side(start, step).start()

                @pl.when(inside & onward)
                def _():
                    on_line(start, step, move).start()

        if distance == 1:
            for peer in range(1, columns):
                to_expert(peer).wait_recv()
                for hop in range(1, groups):
                    pass_on(peer, hop).start()

    own_cot.wait()
    own_rows.wait()
    for step in range(1, groups):
        to_group(step).wait_send()
    for peer in range(1, columns):
        to_expert(peer).wait_send()
    for step in range(groups):
        for start in range(depth):
            to_side(start, step).wait()

            @pl.when((level < depth - 1) & (level >= start))
            def _():
                on_line(start, step, 1).wait_send()

            @pl.when((level > 0) & (level <= start))
            def _():
                on_line(start, step, -1).wait_send()

    for hop in range(1, groups):
        for peer in range(columns):
            pass_on(peer, hop).wait()


def gathered(hidden, routes, gates, cotangent, weight):
    tokens, top, width = hidden.shape
    columns, groups = lax.axis_size("expert"), lax.axis_size("dp")
    capacity = min(tokens, 2 * tokens * top // columns)
    slots = tokens * top
    part = cotangent.shape[1] // groups
    quarters = cotangent.reshape(tokens, groups, part).transpose(1, 0, 2)

    flat = routes.reshape(slots)
    named = (flat[:, None] == jnp.arange(columns, dtype=jnp.int32)[None, :]).astype(jnp.int32)
    position = jnp.sum((jnp.cumsum(named, axis=0) - named) * named, axis=1)
    destination = flat * capacity + position
    places = jnp.arange(columns * capacity, dtype=jnp.int32)
    choose = (places[:, None] == destination[None, :]).astype(jnp.bfloat16)
    by_slot = destination.reshape(tokens, top)
    token_of = sum(
        (places[:, None] == by_slot[None, :, slot]).astype(jnp.bfloat16) for slot in range(top)
    )
    scaled = (
        (gates[:, :, None] * hidden.astype(jnp.float32)).astype(jnp.bfloat16).reshape(slots, width)
    )
    packed = jnp.concatenate(
        [jnp.dot(choose, scaled, preferred_element_type=jnp.float32).astype(jnp.bfloat16), token_of], axis=1
    ).reshape(columns, capacity, width + tokens)

    sems = pltpu.SemaphoreType.DMA
    depth = columns // 2
    every, rows = pl.pallas_call(
        functools.partial(exchange, groups, columns),
        out_shape=(
            jax.ShapeDtypeStruct((groups, columns, tokens, part), jnp.bfloat16),
            jax.ShapeDtypeStruct((groups, columns, capacity, width + tokens), jnp.bfloat16),
        ),
        in_specs=[pl.BlockSpec(memory_space=pl.ANY)] * 2,
        out_specs=[pl.BlockSpec(memory_space=pl.ANY)] * 2,
        scratch_shapes=[
            sems((2,)),
            sems((groups,)),
            sems((groups,)),
            sems((depth, groups)),
            sems((depth, groups)),
            sems((depth, groups)),
            sems((depth, groups)),
            sems((depth, groups)),
            sems((columns,)),
            sems((columns,)),
            sems((groups, columns)),
            sems((groups, columns)),
        ],
        compiler_params=pltpu.CompilerParams(collective_id=0, has_side_effects=True),
        name="exchange",
    )(quarters, packed)

    blocks = groups * columns
    sent, token_of = rows[..., :width], rows[..., width:]
    cot = lax.dot_general(
        token_of.reshape(blocks, capacity, tokens),
        every.reshape(blocks, tokens, part),
        (((2,), (1,)), ((0,), (0,))),
        preferred_element_type=jnp.float32,
    ).astype(jnp.bfloat16).reshape(blocks * capacity, part)
    partial_back = lax.dot_general(
        cot, weight[0], (((1,), (1,)), ((), ())), preferred_element_type=jnp.float32
    ).astype(jnp.bfloat16)
    partial_back = partial_back.reshape(groups, columns, capacity, width)
    summed = lax.psum_scatter(partial_back, "dp", scatter_dimension=0, tiled=True)
    grad_matrix = lax.dot_general(
        sent.reshape(blocks * capacity, width), cot, (((0,), (0,)), ((), ())), preferred_element_type=jnp.float32
    )
    returned = lax.all_to_all(summed[0], "expert", split_axis=0, concat_axis=0, tiled=True)
    back = lax.dot_general(
        choose, returned.reshape(columns * capacity, width), (((0,), (0,)), ((), ())), preferred_element_type=jnp.float32
    )
    grad_hidden = (
        (gates.reshape(slots)[:, None] * back).astype(jnp.bfloat16).reshape(tokens, top, width)
    )
    grad_gates = jnp.sum(
        hidden.reshape(slots, width).astype(jnp.float32) * back, axis=1
    ).reshape(tokens, top)
    return (grad_hidden, grad_gates, grad_matrix.astype(jnp.bfloat16)[None])


def dispatched(hidden, routes, gates, cotangent, weight):
    local_tokens, top_count, hidden_width = hidden.shape
    columns = lax.axis_size("expert")
    capacity = min(local_tokens, 2 * local_tokens * top_count // columns)
    slot_count = local_tokens * top_count
    flat_experts = routes.reshape(slot_count)
    one_hot = (flat_experts[:, None] == jnp.arange(columns, dtype=jnp.int32)[None, :]).astype(
        jnp.int32
    )
    earlier = jnp.cumsum(one_hot, axis=0) - one_hot
    position = jnp.sum(earlier * one_hot, axis=1)
    destination = flat_experts * capacity + position
    slot_of = (
        jnp.full((columns * capacity,), slot_count, jnp.int32)
        .at[destination]
        .set(jnp.arange(slot_count, dtype=jnp.int32))
    )
    scaled = (
        (gates[:, :, None] * hidden.astype(jnp.float32))
        .astype(jnp.bfloat16)
        .reshape(slot_count, hidden_width)
    )
    scaled = jnp.concatenate([scaled, jnp.zeros((1, hidden_width), jnp.bfloat16)], axis=0)
    cot_pad = jnp.concatenate([cotangent, jnp.zeros((1, cotangent.shape[1]), jnp.bfloat16)], axis=0)
    send_rows = scaled[slot_of].reshape(columns, capacity, hidden_width)
    send_cot = cot_pad[slot_of // top_count].reshape(columns, capacity, cotangent.shape[1])
    got_rows, got_cot = (
        lax.all_to_all(send_rows, "expert", split_axis=0, concat_axis=0, tiled=True),
        lax.all_to_all(send_cot, "expert", split_axis=0, concat_axis=0, tiled=True),
    )
    cot_quarter = lax.all_to_all(got_cot[None], "dp", split_axis=3, concat_axis=0, tiled=True)
    rows_all = lax.all_gather(got_rows[None], "dp", axis=0, tiled=True)
    matrix = weight[0]
    partial_back = jnp.einsum(
        "bscd,fd->bscf", cot_quarter, matrix, preferred_element_type=jnp.float32
    )
    summed = lax.psum_scatter(partial_back, "dp", scatter_dimension=0, tiled=True)
    grad_matrix = jnp.einsum(
        "bscf,bscd->fd", rows_all, cot_quarter, preferred_element_type=jnp.float32
    )
    returned = lax.all_to_all(summed[0], "expert", split_axis=0, concat_axis=0, tiled=True)
    back = returned.reshape(columns * capacity, hidden_width)[destination]
    grad_hidden = (
        (gates.reshape(slot_count)[:, None] * back)
        .astype(jnp.bfloat16)
        .reshape(local_tokens, top_count, hidden_width)
    )
    grad_gates = jnp.sum(
        hidden.reshape(slot_count, hidden_width).astype(jnp.float32) * back, axis=1
    ).reshape(local_tokens, top_count)
    return (grad_hidden, grad_gates, grad_matrix.astype(jnp.bfloat16)[None])


def per_device(hidden, routes, gates, cotangent, weight):
    tokens, top = routes.shape
    capacity = min(tokens, 2 * tokens * top // lax.axis_size("expert"))
    form = gathered if tokens <= 2 * capacity else dispatched
    return form(hidden, routes, gates, cotangent, weight)


def solution(mesh):
    placed = (
        P(("dp", "expert"), None, None),
        P(("dp", "expert"), None),
        P(("dp", "expert"), None),
        P(("dp", "expert"), None),
        P("expert", None, "dp"),
    )
    return jax.shard_map(
        per_device,
        mesh=mesh,
        in_specs=placed,
        out_specs=(
            P(("dp", "expert"), None, None),
            P(("dp", "expert"), None),
            P("expert", None, "dp"),
        ),
        check_vma=False,
    )
```

```python
import functools

import jax
import jax.numpy as jnp
from jax import lax
from jax.experimental import pallas as pl
from jax.experimental.pallas import tpu as pltpu
from jax.sharding import PartitionSpec as P

MESH = pl.DeviceIdType.MESH


def exchange(groups, columns, quarters, packed, every, rows, local_sem, dp_send, dp_recv, side_send,
             up_send, down_send, line_recv, side_recv, rows_send, rows_recv, pass_send, pass_recv):
    group, mine = lax.axis_index("dp"), lax.axis_index("expert")
    depth = columns // 2
    level, core = mine // 2, lax.rem(mine, 2)

    def other(index, step, size):
        return lax.rem(index + step, size)

    barrier = pltpu.get_barrier_semaphore()
    for step in range(1, groups):
        pl.semaphore_signal(barrier, inc=1, device_id=(other(group, step, groups), mine), device_id_type=MESH)
    for step in range(1, columns):
        pl.semaphore_signal(barrier, inc=1, device_id=(group, other(mine, step, columns)), device_id_type=MESH)
    pl.semaphore_wait(barrier, groups + columns - 2)

    def remote(source, target, send, recv, device):
        return pltpu.make_async_remote_copy(
            src_ref=source, dst_ref=target, send_sem=send, recv_sem=recv, device_id=device, device_id_type=MESH
        )

    def to_group(step):
        there = other(group, step, groups)
        return remote(quarters.at[there], every.at[mine, group], dp_send.at[step], dp_recv.at[step], (there, mine))

    def to_expert(step):
        there = other(mine, step, columns)
        return remote(packed.at[there], rows.at[mine, group], rows_send.at[step], rows_recv.at[step], (group, there))

    def chunk(start, step):
        source = lax.rem(group - step + groups, groups)
        place = every.at[start * 2 + core, source]
        return place, source

    def on_line(start, step, move, first=False):
        place, source = chunk(start, step)
        send = (up_send if move > 0 else down_send).at[start, step]
        origin = quarters.at[group] if first else place
        return remote(origin, place, send, line_recv.at[start, step], (group, (level + move) * 2 + core))

    def to_side(start, step, first=False):
        place, source = chunk(start, step)
        origin = quarters.at[group] if first else place
        return remote(origin, place, side_send.at[start, step], side_recv.at[start, step], (group, level * 2 + 1 - core))

    def pass_on(step, hop):
        start = lax.rem(mine - step + columns, columns)
        place = rows.at[start, group]
        origin = packed.at[mine] if step == 0 else place
        return remote(origin, place, pass_send.at[hop, step], pass_recv.at[hop, step], (other(group, hop, groups), mine))

    own_cot = pltpu.make_async_copy(quarters.at[group], every.at[mine, group], local_sem.at[0])
    own_rows = pltpu.make_async_copy(packed.at[mine], rows.at[mine, group], local_sem.at[1])

    for step in range(1, groups):
        to_group(step).start()
    for step in range(groups):
        if step:
            to_group(step).wait_recv()
        first = step == 0

        @pl.when(level < depth - 1)
        def _():
            on_line(level, step, 1, first).start()

        @pl.when(level > 0)
        def _():
            on_line(level, step, -1, first).start()

        to_side(level, step, first).start()
        if first:
            own_cot.start()
            own_rows.start()
            for peer in range(1, columns):
                to_expert(peer).start()
            for hop in range(1, groups):
                pass_on(0, hop).start()
    for distance in range(1, depth):
        for step in range(groups):
            for move in (1, -1):
                start = level - move * distance
                inside = (start >= 0) & (start < depth)
                onward = (level < depth - 1) if move > 0 else (level > 0)

                @pl.when(inside)
                def _():
                    on_line(start, step, move).wait_recv()
                    to_side(start, step).start()

                @pl.when(inside & onward)
                def _():
                    on_line(start, step, move).start()

        if distance == 1:
            for peer in range(1, columns):
                to_expert(peer).wait_recv()
                for hop in range(1, groups):
                    pass_on(peer, hop).start()

    own_cot.wait()
    own_rows.wait()
    for step in range(1, groups):
        to_group(step).wait_send()
    for peer in range(1, columns):
        to_expert(peer).wait_send()
    for step in range(groups):
        for start in range(depth):
            to_side(start, step).wait()

            @pl.when((level < depth - 1) & (level >= start))
            def _():
                on_line(start, step, 1).wait_send()

            @pl.when((level > 0) & (level <= start))
            def _():
                on_line(start, step, -1).wait_send()

    for hop in range(1, groups):
        for peer in range(columns):
            pass_on(peer, hop).wait()


def product(groups, columns, cot, matrix, sent, grad, back, partial, arrived, total,
            part_send, part_recv, back_send, back_recv):
    group, mine = lax.axis_index("dp"), lax.axis_index("expert")
    capacity, width = total.shape[1:]
    part = cot.shape[-1]

    barrier = pltpu.get_barrier_semaphore()
    for step in range(1, groups):
        pl.semaphore_signal(barrier, inc=1, device_id=(lax.rem(group + step, groups), mine), device_id_type=MESH)
    for step in range(1, columns):
        pl.semaphore_signal(barrier, inc=1, device_id=(group, lax.rem(mine + step, columns)), device_id_type=MESH)
    pl.semaphore_wait(barrier, groups + columns - 2)

    def to_group(turn, step):
        there = lax.rem(group + step, groups)
        return pltpu.make_async_remote_copy(
            src_ref=partial.at[turn, there],
            dst_ref=arrived.at[step, turn],
            send_sem=part_send.at[step, turn],
            recv_sem=part_recv.at[step, turn],
            device_id=(there, mine),
            device_id_type=MESH,
        )

    def to_expert(turn):
        return pltpu.make_async_remote_copy(
            src_ref=total.at[turn],
            dst_ref=back.at[mine],
            send_sem=back_send.at[turn],
            recv_sem=back_recv.at[turn],
            device_id=(group, lax.rem(mine + turn + 1, columns)),
            device_id_type=MESH,
        )

    def multiply(turn, carry):
        there = lax.rem(mine + turn + 1, columns)
        block = cot[there].reshape(groups * capacity, part)
        terms = lax.dot_general(block, matrix[...], (((1,), (1,)), ((), ())), preferred_element_type=jnp.float32)
        partial[turn] = terms.astype(jnp.bfloat16).reshape(groups, capacity, width)
        for step in range(1, groups):
            to_group(turn, step).start()
        return carry

    lax.fori_loop(0, columns, multiply, 0)

    span = 256
    slots = columns * groups * capacity

    def outer(tile, carry):
        at = pl.ds(pl.multiple_of(tile * span, span), span)
        block = cot[:, :, :, at].reshape(slots, span)
        grad[:, at] = jnp.dot(sent[...], block, preferred_element_type=jnp.float32).astype(jnp.bfloat16)
        return carry

    lax.fori_loop(0, part // span, outer, 0)

    def add(turn):
        for step in range(1, groups):
            to_group(turn, step).wait_recv()
        value = partial[turn, group].astype(jnp.float32)
        for step in range(1, groups):
            value = value + arrived[step, turn].astype(jnp.float32)
        return value.astype(jnp.bfloat16)

    def hand_back(turn, carry):
        total[turn] = add(turn)
        to_expert(turn).start()
        return carry

    lax.fori_loop(0, columns - 1, hand_back, 0)
    back[mine] = add(columns - 1)

    def finish(turn, carry):
        for step in range(1, groups):
            to_group(turn, step).wait_send()
        return carry

    lax.fori_loop(0, columns, finish, 0)

    def arrive(turn, carry):
        to_expert(turn).wait()
        return carry

    lax.fori_loop(0, columns - 1, arrive, 0)


def gathered(hidden, routes, gates, cotangent, weight):
    tokens, top, width = hidden.shape
    columns, groups = lax.axis_size("expert"), lax.axis_size("dp")
    capacity = min(tokens, 2 * tokens * top // columns)
    slots = tokens * top
    part = cotangent.shape[1] // groups
    quarters = cotangent.reshape(tokens, groups, part).transpose(1, 0, 2)

    flat = routes.reshape(slots)
    named = (flat[:, None] == jnp.arange(columns, dtype=jnp.int32)[None, :]).astype(jnp.int32)
    position = jnp.sum((jnp.cumsum(named, axis=0) - named) * named, axis=1)
    destination = flat * capacity + position
    places = jnp.arange(columns * capacity, dtype=jnp.int32)
    choose = (places[:, None] == destination[None, :]).astype(jnp.bfloat16)
    by_slot = destination.reshape(tokens, top)
    token_of = sum(
        (places[:, None] == by_slot[None, :, slot]).astype(jnp.bfloat16) for slot in range(top)
    )
    scaled = (
        (gates[:, :, None] * hidden.astype(jnp.float32)).astype(jnp.bfloat16).reshape(slots, width)
    )
    packed = jnp.concatenate(
        [jnp.dot(choose, scaled, preferred_element_type=jnp.float32).astype(jnp.bfloat16), token_of], axis=1
    ).reshape(columns, capacity, width + tokens)

    sems = pltpu.SemaphoreType.DMA
    depth = columns // 2
    every, rows = pl.pallas_call(
        functools.partial(exchange, groups, columns),
        out_shape=(
            jax.ShapeDtypeStruct((columns, groups, tokens, part), jnp.bfloat16),
            jax.ShapeDtypeStruct((columns, groups, capacity, width + tokens), jnp.bfloat16),
        ),
        in_specs=[pl.BlockSpec(memory_space=pl.ANY)] * 2,
        out_specs=[pl.BlockSpec(memory_space=pl.ANY)] * 2,
        scratch_shapes=[
            sems((2,)),
            sems((groups,)),
            sems((groups,)),
            sems((depth, groups)),
            sems((depth, groups)),
            sems((depth, groups)),
            sems((depth, groups)),
            sems((depth, groups)),
            sems((columns,)),
            sems((columns,)),
            sems((groups, columns)),
            sems((groups, columns)),
        ],
        compiler_params=pltpu.CompilerParams(collective_id=0, has_side_effects=True),
        name="exchange",
    )(quarters, packed)

    blocks = groups * columns
    token_of = rows[..., width:]
    cot = lax.dot_general(
        token_of.reshape(blocks, capacity, tokens),
        every.reshape(blocks, tokens, part),
        (((2,), (1,)), ((0,), (0,))),
        preferred_element_type=jnp.float32,
    ).astype(jnp.bfloat16).reshape(columns, groups, capacity, part)
    sent = rows[..., :width].reshape(blocks * capacity, width).T
    grad_matrix, returned = pl.pallas_call(
        functools.partial(product, groups, columns),
        out_shape=(
            jax.ShapeDtypeStruct((width, part), jnp.bfloat16),
            jax.ShapeDtypeStruct((columns, capacity, width), jnp.bfloat16),
        ),
        in_specs=[pl.BlockSpec(memory_space=pltpu.VMEM)] * 3,
        out_specs=[pl.BlockSpec(memory_space=pltpu.VMEM)] * 2,
        scratch_shapes=[
            pltpu.VMEM((columns, groups, capacity, width), jnp.bfloat16),
            pltpu.VMEM((groups, columns, capacity, width), jnp.bfloat16),
            pltpu.VMEM((columns, capacity, width), jnp.bfloat16),
            sems((groups, columns)),
            sems((groups, columns)),
            sems((columns,)),
            sems((columns,)),
        ],
        compiler_params=pltpu.CompilerParams(
            collective_id=1, has_side_effects=True, vmem_limit_bytes=56 << 20
        ),
        name="product",
    )(cot, weight[0], sent)
    back = lax.dot_general(
        choose, returned.reshape(columns * capacity, width), (((0,), (0,)), ((), ())), preferred_element_type=jnp.float32
    )
    grad_hidden = (
        (gates.reshape(slots)[:, None] * back).astype(jnp.bfloat16).reshape(tokens, top, width)
    )
    grad_gates = jnp.sum(
        hidden.reshape(slots, width).astype(jnp.float32) * back, axis=1
    ).reshape(tokens, top)
    return (grad_hidden, grad_gates, grad_matrix[None])


def dispatched(hidden, routes, gates, cotangent, weight):
    local_tokens, top_count, hidden_width = hidden.shape
    columns = lax.axis_size("expert")
    capacity = min(local_tokens, 2 * local_tokens * top_count // columns)
    slot_count = local_tokens * top_count
    flat_experts = routes.reshape(slot_count)
    one_hot = (flat_experts[:, None] == jnp.arange(columns, dtype=jnp.int32)[None, :]).astype(
        jnp.int32
    )
    earlier = jnp.cumsum(one_hot, axis=0) - one_hot
    position = jnp.sum(earlier * one_hot, axis=1)
    destination = flat_experts * capacity + position
    slot_of = (
        jnp.full((columns * capacity,), slot_count, jnp.int32)
        .at[destination]
        .set(jnp.arange(slot_count, dtype=jnp.int32))
    )
    scaled = (
        (gates[:, :, None] * hidden.astype(jnp.float32))
        .astype(jnp.bfloat16)
        .reshape(slot_count, hidden_width)
    )
    scaled = jnp.concatenate([scaled, jnp.zeros((1, hidden_width), jnp.bfloat16)], axis=0)
    cot_pad = jnp.concatenate([cotangent, jnp.zeros((1, cotangent.shape[1]), jnp.bfloat16)], axis=0)
    send_rows = scaled[slot_of].reshape(columns, capacity, hidden_width)
    send_cot = cot_pad[slot_of // top_count].reshape(columns, capacity, cotangent.shape[1])
    got_rows, got_cot = (
        lax.all_to_all(send_rows, "expert", split_axis=0, concat_axis=0, tiled=True),
        lax.all_to_all(send_cot, "expert", split_axis=0, concat_axis=0, tiled=True),
    )
    cot_quarter = lax.all_to_all(got_cot[None], "dp", split_axis=3, concat_axis=0, tiled=True)
    rows_all = lax.all_gather(got_rows[None], "dp", axis=0, tiled=True)
    matrix = weight[0]
    partial_back = jnp.einsum(
        "bscd,fd->bscf", cot_quarter, matrix, preferred_element_type=jnp.float32
    )
    summed = lax.psum_scatter(partial_back, "dp", scatter_dimension=0, tiled=True)
    grad_matrix = jnp.einsum(
        "bscf,bscd->fd", rows_all, cot_quarter, preferred_element_type=jnp.float32
    )
    returned = lax.all_to_all(summed[0], "expert", split_axis=0, concat_axis=0, tiled=True)
    back = returned.reshape(columns * capacity, hidden_width)[destination]
    grad_hidden = (
        (gates.reshape(slot_count)[:, None] * back)
        .astype(jnp.bfloat16)
        .reshape(local_tokens, top_count, hidden_width)
    )
    grad_gates = jnp.sum(
        hidden.reshape(slot_count, hidden_width).astype(jnp.float32) * back, axis=1
    ).reshape(local_tokens, top_count)
    return (grad_hidden, grad_gates, grad_matrix.astype(jnp.bfloat16)[None])


def per_device(hidden, routes, gates, cotangent, weight):
    tokens, top = routes.shape
    capacity = min(tokens, 2 * tokens * top // lax.axis_size("expert"))
    form = gathered if tokens <= 2 * capacity else dispatched
    return form(hidden, routes, gates, cotangent, weight)


def solution(mesh):
    placed = (
        P(("dp", "expert"), None, None),
        P(("dp", "expert"), None),
        P(("dp", "expert"), None),
        P(("dp", "expert"), None),
        P("expert", None, "dp"),
    )
    return jax.shard_map(
        per_device,
        mesh=mesh,
        in_specs=placed,
        out_specs=(
            P(("dp", "expert"), None, None),
            P(("dp", "expert"), None),
            P("expert", None, "dp"),
        ),
        check_vma=False,
    )
```

```python
import functools

import jax
import jax.numpy as jnp
from jax import lax
from jax.experimental import pallas as pl
from jax.experimental.pallas import tpu as pltpu
from jax.sharding import PartitionSpec as P

MESH = pl.DeviceIdType.MESH


def exchange(groups, columns, quarters, packed, every, rows, local_sem, dp_send, dp_recv, side_send,
             up_send, down_send, line_recv, side_recv, rows_send, rows_recv, pass_send, pass_recv):
    group, mine = lax.axis_index("dp"), lax.axis_index("expert")
    depth = columns // 2
    level, core = mine // 2, lax.rem(mine, 2)

    def other(index, step, size):
        return lax.rem(index + step, size)

    barrier = pltpu.get_barrier_semaphore()
    for step in range(1, groups):
        pl.semaphore_signal(barrier, inc=1, device_id=(other(group, step, groups), mine), device_id_type=MESH)
    for step in range(1, columns):
        pl.semaphore_signal(barrier, inc=1, device_id=(group, other(mine, step, columns)), device_id_type=MESH)
    pl.semaphore_wait(barrier, groups + columns - 2)

    def remote(source, target, send, recv, device):
        return pltpu.make_async_remote_copy(
            src_ref=source, dst_ref=target, send_sem=send, recv_sem=recv, device_id=device, device_id_type=MESH
        )

    def to_group(step):
        there = other(group, step, groups)
        return remote(quarters.at[there], every.at[mine, group], dp_send.at[step], dp_recv.at[step], (there, mine))

    def to_expert(step):
        there = other(mine, step, columns)
        return remote(packed.at[there], rows.at[mine, group], rows_send.at[step], rows_recv.at[step], (group, there))

    def chunk(start, step):
        source = lax.rem(group - step + groups, groups)
        place = every.at[start * 2 + core, source]
        return place, source

    def on_line(start, step, move, first=False):
        place, source = chunk(start, step)
        send = (up_send if move > 0 else down_send).at[start, step]
        origin = quarters.at[group] if first else place
        return remote(origin, place, send, line_recv.at[start, step], (group, (level + move) * 2 + core))

    def to_side(start, step, first=False):
        place, source = chunk(start, step)
        origin = quarters.at[group] if first else place
        return remote(origin, place, side_send.at[start, step], side_recv.at[start, step], (group, level * 2 + 1 - core))

    def pass_on(step, hop):
        start = lax.rem(mine - step + columns, columns)
        place = rows.at[start, group]
        origin = packed.at[mine] if step == 0 else place
        return remote(origin, place, pass_send.at[hop, step], pass_recv.at[hop, step], (other(group, hop, groups), mine))

    own_cot = pltpu.make_async_copy(quarters.at[group], every.at[mine, group], local_sem.at[0])
    own_rows = pltpu.make_async_copy(packed.at[mine], rows.at[mine, group], local_sem.at[1])

    for step in range(1, groups):
        to_group(step).start()
    for step in range(groups):
        if step:
            to_group(step).wait_recv()
        first = step == 0

        @pl.when(level < depth - 1)
        def _():
            on_line(level, step, 1, first).start()

        @pl.when(level > 0)
        def _():
            on_line(level, step, -1, first).start()

        to_side(level, step, first).start()
        if first:
            own_cot.start()
            own_rows.start()
            for peer in range(1, columns):
                to_expert(peer).start()
            for hop in range(1, groups):
                pass_on(0, hop).start()
    for distance in range(1, depth):
        for step in range(groups):
            for move in (1, -1):
                start = level - move * distance
                inside = (start >= 0) & (start < depth)
                onward = (level < depth - 1) if move > 0 else (level > 0)

                @pl.when(inside)
                def _():
                    on_line(start, step, move).wait_recv()
                    to_side(start, step).start()

                @pl.when(inside & onward)
                def _():
                    on_line(start, step, move).start()

        if distance == 1:
            for peer in range(1, columns):
                to_expert(peer).wait_recv()
                for hop in range(1, groups):
                    pass_on(peer, hop).start()

    own_cot.wait()
    own_rows.wait()
    for step in range(1, groups):
        to_group(step).wait_send()
    for peer in range(1, columns):
        to_expert(peer).wait_send()
    for step in range(groups):
        for start in range(depth):
            to_side(start, step).wait()

            @pl.when((level < depth - 1) & (level >= start))
            def _():
                on_line(start, step, 1).wait_send()

            @pl.when((level > 0) & (level <= start))
            def _():
                on_line(start, step, -1).wait_send()

    for hop in range(1, groups):
        for peer in range(columns):
            pass_on(peer, hop).wait()


def product(groups, columns, every, matrix, rows, grad, back, cot, sent, chunk, partial, arrived, total,
            part_send, part_recv, back_send, back_recv, chunk_sem):
    group, mine = lax.axis_index("dp"), lax.axis_index("expert")
    capacity, width = total.shape[1:]
    part = cot.shape[-1]

    def fetch(turn):
        there, slot = lax.rem(mine + turn + 1, columns), lax.rem(turn, 2)
        return pltpu.make_async_copy(every.at[there], chunk.at[slot], chunk_sem.at[slot])

    fetch(0).start()
    barrier = pltpu.get_barrier_semaphore()
    for step in range(1, groups):
        pl.semaphore_signal(barrier, inc=1, device_id=(lax.rem(group + step, groups), mine), device_id_type=MESH)
    for step in range(1, columns):
        pl.semaphore_signal(barrier, inc=1, device_id=(group, lax.rem(mine + step, columns)), device_id_type=MESH)
    pl.semaphore_wait(barrier, groups + columns - 2)

    def to_group(turn, step):
        there = lax.rem(group + step, groups)
        return pltpu.make_async_remote_copy(
            src_ref=partial.at[turn, there],
            dst_ref=arrived.at[step, turn],
            send_sem=part_send.at[step, turn],
            recv_sem=part_recv.at[step, turn],
            device_id=(there, mine),
            device_id_type=MESH,
        )

    def to_expert(turn):
        return pltpu.make_async_remote_copy(
            src_ref=total.at[turn],
            dst_ref=back.at[mine],
            send_sem=back_send.at[turn],
            recv_sem=back_recv.at[turn],
            device_id=(group, lax.rem(mine + turn + 1, columns)),
            device_id_type=MESH,
        )

    def multiply(turn, carry):
        there = lax.rem(mine + turn + 1, columns)
        slot = lax.rem(turn, 2)

        @pl.when(turn + 1 < columns)
        def _():
            fetch(turn + 1).start()

        fetch(turn).wait()
        for source in range(groups):
            picked = jnp.dot(rows[there, source, :, width:], chunk[slot, source], preferred_element_type=jnp.float32)
            cot[there, source] = picked.astype(jnp.bfloat16)
        block = cot[there].reshape(groups * capacity, part)
        terms = lax.dot_general(block, matrix[...], (((1,), (1,)), ((), ())), preferred_element_type=jnp.float32)
        partial[turn] = terms.astype(jnp.bfloat16).reshape(groups, capacity, width)
        for step in range(1, groups):
            to_group(turn, step).start()
        return carry

    lax.fori_loop(0, columns, multiply, 0)

    for start in range(columns):
        at = pl.ds(start * groups * capacity, groups * capacity)
        sent[:, at] = rows[start, :, :, :width].reshape(groups * capacity, width).T

    span = 256
    slots = columns * groups * capacity

    def outer(tile, carry):
        at = pl.ds(pl.multiple_of(tile * span, span), span)
        block = cot[:, :, :, at].reshape(slots, span)
        grad[:, at] = jnp.dot(sent[...], block, preferred_element_type=jnp.float32).astype(jnp.bfloat16)
        return carry

    lax.fori_loop(0, part // span, outer, 0)

    def add(turn):
        for step in range(1, groups):
            to_group(turn, step).wait_recv()
        value = partial[turn, group].astype(jnp.float32)
        for step in range(1, groups):
            value = value + arrived[step, turn].astype(jnp.float32)
        return value.astype(jnp.bfloat16)

    def hand_back(turn, carry):
        total[turn] = add(turn)
        to_expert(turn).start()
        return carry

    lax.fori_loop(0, columns - 1, hand_back, 0)
    back[mine] = add(columns - 1)

    def finish(turn, carry):
        for step in range(1, groups):
            to_group(turn, step).wait_send()
        return carry

    lax.fori_loop(0, columns, finish, 0)

    def arrive(turn, carry):
        to_expert(turn).wait()
        return carry

    lax.fori_loop(0, columns - 1, arrive, 0)


def gathered(hidden, routes, gates, cotangent, weight):
    tokens, top, width = hidden.shape
    columns, groups = lax.axis_size("expert"), lax.axis_size("dp")
    capacity = min(tokens, 2 * tokens * top // columns)
    slots = tokens * top
    part = cotangent.shape[1] // groups
    quarters = cotangent.reshape(tokens, groups, part).transpose(1, 0, 2)

    flat = routes.reshape(slots)
    named = (flat[:, None] == jnp.arange(columns, dtype=jnp.int32)[None, :]).astype(jnp.int32)
    position = jnp.sum((jnp.cumsum(named, axis=0) - named) * named, axis=1)
    destination = flat * capacity + position
    places = jnp.arange(columns * capacity, dtype=jnp.int32)
    choose = (places[:, None] == destination[None, :]).astype(jnp.bfloat16)
    by_slot = destination.reshape(tokens, top)
    token_of = sum(
        (places[:, None] == by_slot[None, :, slot]).astype(jnp.bfloat16) for slot in range(top)
    )
    scaled = (
        (gates[:, :, None] * hidden.astype(jnp.float32)).astype(jnp.bfloat16).reshape(slots, width)
    )
    packed = jnp.concatenate(
        [jnp.dot(choose, scaled, preferred_element_type=jnp.float32).astype(jnp.bfloat16), token_of], axis=1
    ).reshape(columns, capacity, width + tokens)

    sems = pltpu.SemaphoreType.DMA
    depth = columns // 2
    every, rows = pl.pallas_call(
        functools.partial(exchange, groups, columns),
        out_shape=(
            jax.ShapeDtypeStruct((columns, groups, tokens, part), jnp.bfloat16),
            jax.ShapeDtypeStruct((columns, groups, capacity, width + tokens), jnp.bfloat16),
        ),
        in_specs=[pl.BlockSpec(memory_space=pl.ANY)] * 2,
        out_specs=[pl.BlockSpec(memory_space=pl.ANY)] * 2,
        scratch_shapes=[
            sems((2,)),
            sems((groups,)),
            sems((groups,)),
            sems((depth, groups)),
            sems((depth, groups)),
            sems((depth, groups)),
            sems((depth, groups)),
            sems((depth, groups)),
            sems((columns,)),
            sems((columns,)),
            sems((groups, columns)),
            sems((groups, columns)),
        ],
        compiler_params=pltpu.CompilerParams(collective_id=0, has_side_effects=True),
        name="exchange",
    )(quarters, packed)

    grad_matrix, returned = pl.pallas_call(
        functools.partial(product, groups, columns),
        out_shape=(
            jax.ShapeDtypeStruct((width, part), jnp.bfloat16),
            jax.ShapeDtypeStruct((columns, capacity, width), jnp.bfloat16),
        ),
        in_specs=[pl.BlockSpec(memory_space=pl.ANY)] + [pl.BlockSpec(memory_space=pltpu.VMEM)] * 2,
        out_specs=[pl.BlockSpec(memory_space=pltpu.VMEM)] * 2,
        scratch_shapes=[
            pltpu.VMEM((columns, groups, capacity, part), jnp.bfloat16),
            pltpu.VMEM((width, columns * groups * capacity), jnp.bfloat16),
            pltpu.VMEM((2, groups, tokens, part), jnp.bfloat16),
            pltpu.VMEM((columns, groups, capacity, width), jnp.bfloat16),
            pltpu.VMEM((groups, columns, capacity, width), jnp.bfloat16),
            pltpu.VMEM((columns, capacity, width), jnp.bfloat16),
            sems((groups, columns)),
            sems((groups, columns)),
            sems((columns,)),
            sems((columns,)),
            sems((2,)),
        ],
        compiler_params=pltpu.CompilerParams(
            collective_id=1, has_side_effects=True, vmem_limit_bytes=56 << 20
        ),
        name="product",
    )(every, weight[0], rows)
    back = lax.dot_general(
        choose, returned.reshape(columns * capacity, width), (((0,), (0,)), ((), ())), preferred_element_type=jnp.float32
    )
    grad_hidden = (
        (gates.reshape(slots)[:, None] * back).astype(jnp.bfloat16).reshape(tokens, top, width)
    )
    grad_gates = jnp.sum(
        hidden.reshape(slots, width).astype(jnp.float32) * back, axis=1
    ).reshape(tokens, top)
    return (grad_hidden, grad_gates, grad_matrix[None])


def dispatched(hidden, routes, gates, cotangent, weight):
    local_tokens, top_count, hidden_width = hidden.shape
    columns = lax.axis_size("expert")
    capacity = min(local_tokens, 2 * local_tokens * top_count // columns)
    slot_count = local_tokens * top_count
    flat_experts = routes.reshape(slot_count)
    one_hot = (flat_experts[:, None] == jnp.arange(columns, dtype=jnp.int32)[None, :]).astype(
        jnp.int32
    )
    earlier = jnp.cumsum(one_hot, axis=0) - one_hot
    position = jnp.sum(earlier * one_hot, axis=1)
    destination = flat_experts * capacity + position
    slot_of = (
        jnp.full((columns * capacity,), slot_count, jnp.int32)
        .at[destination]
        .set(jnp.arange(slot_count, dtype=jnp.int32))
    )
    scaled = (
        (gates[:, :, None] * hidden.astype(jnp.float32))
        .astype(jnp.bfloat16)
        .reshape(slot_count, hidden_width)
    )
    scaled = jnp.concatenate([scaled, jnp.zeros((1, hidden_width), jnp.bfloat16)], axis=0)
    cot_pad = jnp.concatenate([cotangent, jnp.zeros((1, cotangent.shape[1]), jnp.bfloat16)], axis=0)
    send_rows = scaled[slot_of].reshape(columns, capacity, hidden_width)
    send_cot = cot_pad[slot_of // top_count].reshape(columns, capacity, cotangent.shape[1])
    got_rows, got_cot = (
        lax.all_to_all(send_rows, "expert", split_axis=0, concat_axis=0, tiled=True),
        lax.all_to_all(send_cot, "expert", split_axis=0, concat_axis=0, tiled=True),
    )
    cot_quarter = lax.all_to_all(got_cot[None], "dp", split_axis=3, concat_axis=0, tiled=True)
    rows_all = lax.all_gather(got_rows[None], "dp", axis=0, tiled=True)
    matrix = weight[0]
    partial_back = jnp.einsum(
        "bscd,fd->bscf", cot_quarter, matrix, preferred_element_type=jnp.float32
    )
    summed = lax.psum_scatter(partial_back, "dp", scatter_dimension=0, tiled=True)
    grad_matrix = jnp.einsum(
        "bscf,bscd->fd", rows_all, cot_quarter, preferred_element_type=jnp.float32
    )
    returned = lax.all_to_all(summed[0], "expert", split_axis=0, concat_axis=0, tiled=True)
    back = returned.reshape(columns * capacity, hidden_width)[destination]
    grad_hidden = (
        (gates.reshape(slot_count)[:, None] * back)
        .astype(jnp.bfloat16)
        .reshape(local_tokens, top_count, hidden_width)
    )
    grad_gates = jnp.sum(
        hidden.reshape(slot_count, hidden_width).astype(jnp.float32) * back, axis=1
    ).reshape(local_tokens, top_count)
    return (grad_hidden, grad_gates, grad_matrix.astype(jnp.bfloat16)[None])


def per_device(hidden, routes, gates, cotangent, weight):
    tokens, top = routes.shape
    capacity = min(tokens, 2 * tokens * top // lax.axis_size("expert"))
    form = gathered if tokens <= 2 * capacity else dispatched
    return form(hidden, routes, gates, cotangent, weight)


def solution(mesh):
    placed = (
        P(("dp", "expert"), None, None),
        P(("dp", "expert"), None),
        P(("dp", "expert"), None),
        P(("dp", "expert"), None),
        P("expert", None, "dp"),
    )
    return jax.shard_map(
        per_device,
        mesh=mesh,
        in_specs=placed,
        out_specs=(
            P(("dp", "expert"), None, None),
            P(("dp", "expert"), None),
            P("expert", None, "dp"),
        ),
        check_vma=False,
    )
```

```python
import functools

import jax
import jax.numpy as jnp
from jax import lax
from jax.experimental import pallas as pl
from jax.experimental.pallas import tpu as pltpu
from jax.sharding import PartitionSpec as P

MESH = pl.DeviceIdType.MESH


def exchange(groups, columns, cotangent, packed, every, rows, local_sem, dp_send, dp_recv, side_send,
             up_send, down_send, line_recv, side_recv, rows_send, rows_recv, pass_send, pass_recv):
    group, mine = lax.axis_index("dp"), lax.axis_index("expert")
    depth = columns // 2
    level, core = mine // 2, lax.rem(mine, 2)

    part = cotangent.shape[1] // groups

    def quarter(index):
        return cotangent.at[:, pl.ds(pl.multiple_of(index * part, part), part)]

    def other(index, step, size):
        return lax.rem(index + step, size)

    barrier = pltpu.get_barrier_semaphore()
    for step in range(1, groups):
        pl.semaphore_signal(barrier, inc=1, device_id=(other(group, step, groups), mine), device_id_type=MESH)
    for step in range(1, columns):
        pl.semaphore_signal(barrier, inc=1, device_id=(group, other(mine, step, columns)), device_id_type=MESH)
    pl.semaphore_wait(barrier, groups + columns - 2)

    def remote(source, target, send, recv, device):
        return pltpu.make_async_remote_copy(
            src_ref=source, dst_ref=target, send_sem=send, recv_sem=recv, device_id=device, device_id_type=MESH
        )

    def to_group(step):
        there = other(group, step, groups)
        return remote(quarter(there), every.at[mine, group], dp_send.at[step], dp_recv.at[step], (there, mine))

    def to_expert(step):
        there = other(mine, step, columns)
        return remote(packed.at[there], rows.at[mine, group], rows_send.at[step], rows_recv.at[step], (group, there))

    def chunk(start, step):
        source = lax.rem(group - step + groups, groups)
        place = every.at[start * 2 + core, source]
        return place, source

    def on_line(start, step, move, first=False):
        place, source = chunk(start, step)
        send = (up_send if move > 0 else down_send).at[start, step]
        origin = quarter(group) if first else place
        return remote(origin, place, send, line_recv.at[start, step], (group, (level + move) * 2 + core))

    def to_side(start, step, first=False):
        place, source = chunk(start, step)
        origin = quarter(group) if first else place
        return remote(origin, place, side_send.at[start, step], side_recv.at[start, step], (group, level * 2 + 1 - core))

    def pass_on(step, hop):
        start = lax.rem(mine - step + columns, columns)
        place = rows.at[start, group]
        origin = packed.at[mine] if step == 0 else place
        return remote(origin, place, pass_send.at[hop, step], pass_recv.at[hop, step], (other(group, hop, groups), mine))

    own_cot = pltpu.make_async_copy(quarter(group), every.at[mine, group], local_sem.at[0])
    own_rows = pltpu.make_async_copy(packed.at[mine], rows.at[mine, group], local_sem.at[1])

    for step in range(1, groups):
        to_group(step).start()
    for step in range(groups):
        if step:
            to_group(step).wait_recv()
        first = step == 0

        @pl.when(level < depth - 1)
        def _():
            on_line(level, step, 1, first).start()

        @pl.when(level > 0)
        def _():
            on_line(level, step, -1, first).start()

        to_side(level, step, first).start()
        if first:
            own_cot.start()
            own_rows.start()
            for peer in range(1, columns):
                to_expert(peer).start()
            for hop in range(1, groups):
                pass_on(0, hop).start()
    for distance in range(1, depth):
        for step in range(groups):
            for move in (1, -1):
                start = level - move * distance
                inside = (start >= 0) & (start < depth)
                onward = (level < depth - 1) if move > 0 else (level > 0)

                @pl.when(inside)
                def _():
                    on_line(start, step, move).wait_recv()
                    to_side(start, step).start()

                @pl.when(inside & onward)
                def _():
                    on_line(start, step, move).start()

        if distance == 1:
            for peer in range(1, columns):
                to_expert(peer).wait_recv()
                for hop in range(1, groups):
                    pass_on(peer, hop).start()

    own_cot.wait()
    own_rows.wait()
    for step in range(1, groups):
        to_group(step).wait_send()
    for peer in range(1, columns):
        to_expert(peer).wait_send()
    for step in range(groups):
        for start in range(depth):
            to_side(start, step).wait()

            @pl.when((level < depth - 1) & (level >= start))
            def _():
                on_line(start, step, 1).wait_send()

            @pl.when((level > 0) & (level <= start))
            def _():
                on_line(start, step, -1).wait_send()

    for hop in range(1, groups):
        for peer in range(columns):
            pass_on(peer, hop).wait()


def product(groups, columns, every, matrix, rows, grad, back, cot, sent, chunk, partial, arrived, total,
            part_send, part_recv, back_send, back_recv, chunk_sem):
    group, mine = lax.axis_index("dp"), lax.axis_index("expert")
    capacity, width = total.shape[1:]
    part = cot.shape[-1]

    def fetch(turn):
        there, slot = lax.rem(mine + turn + 1, columns), lax.rem(turn, 2)
        return pltpu.make_async_copy(every.at[there], chunk.at[slot], chunk_sem.at[slot])

    fetch(0).start()
    barrier = pltpu.get_barrier_semaphore()
    for step in range(1, groups):
        pl.semaphore_signal(barrier, inc=1, device_id=(lax.rem(group + step, groups), mine), device_id_type=MESH)
    for step in range(1, columns):
        pl.semaphore_signal(barrier, inc=1, device_id=(group, lax.rem(mine + step, columns)), device_id_type=MESH)
    pl.semaphore_wait(barrier, groups + columns - 2)

    def to_group(turn, step):
        there = lax.rem(group + step, groups)
        return pltpu.make_async_remote_copy(
            src_ref=partial.at[turn, there],
            dst_ref=arrived.at[step, turn],
            send_sem=part_send.at[step, turn],
            recv_sem=part_recv.at[step, turn],
            device_id=(there, mine),
            device_id_type=MESH,
        )

    def to_expert(turn):
        return pltpu.make_async_remote_copy(
            src_ref=total.at[turn],
            dst_ref=back.at[mine],
            send_sem=back_send.at[turn],
            recv_sem=back_recv.at[turn],
            device_id=(group, lax.rem(mine + turn + 1, columns)),
            device_id_type=MESH,
        )

    def multiply(turn, carry):
        there = lax.rem(mine + turn + 1, columns)
        slot = lax.rem(turn, 2)

        @pl.when(turn + 1 < columns)
        def _():
            fetch(turn + 1).start()

        fetch(turn).wait()
        for source in range(groups):
            picked = jnp.dot(rows[there, source, :, width:], chunk[slot, source], preferred_element_type=jnp.float32)
            cot[there, source] = picked.astype(jnp.bfloat16)
        block = cot[there].reshape(groups * capacity, part)
        terms = lax.dot_general(block, matrix[...], (((1,), (1,)), ((), ())), preferred_element_type=jnp.float32)
        partial[turn] = terms.astype(jnp.bfloat16).reshape(groups, capacity, width)
        for step in range(1, groups):
            to_group(turn, step).start()
        return carry

    lax.fori_loop(0, columns, multiply, 0)

    for start in range(columns):
        at = pl.ds(start * groups * capacity, groups * capacity)
        sent[:, at] = rows[start, :, :, :width].reshape(groups * capacity, width).T

    span = 256
    slots = columns * groups * capacity

    def outer(tile, carry):
        at = pl.ds(pl.multiple_of(tile * span, span), span)
        block = cot[:, :, :, at].reshape(slots, span)
        grad[:, at] = jnp.dot(sent[...], block, preferred_element_type=jnp.float32).astype(jnp.bfloat16)
        return carry

    lax.fori_loop(0, part // span, outer, 0)

    def add(turn):
        for step in range(1, groups):
            to_group(turn, step).wait_recv()
        value = partial[turn, group].astype(jnp.float32)
        for step in range(1, groups):
            value = value + arrived[step, turn].astype(jnp.float32)
        return value.astype(jnp.bfloat16)

    def hand_back(turn, carry):
        total[turn] = add(turn)
        to_expert(turn).start()
        return carry

    lax.fori_loop(0, columns - 1, hand_back, 0)
    back[mine] = add(columns - 1)

    def finish(turn, carry):
        for step in range(1, groups):
            to_group(turn, step).wait_send()
        return carry

    lax.fori_loop(0, columns, finish, 0)

    def arrive(turn, carry):
        to_expert(turn).wait()
        return carry

    lax.fori_loop(0, columns - 1, arrive, 0)


def gathered(hidden, routes, gates, cotangent, weight):
    tokens, top, width = hidden.shape
    columns, groups = lax.axis_size("expert"), lax.axis_size("dp")
    capacity = min(tokens, 2 * tokens * top // columns)
    slots = tokens * top
    part = cotangent.shape[1] // groups

    flat = routes.reshape(slots)
    named = (flat[:, None] == jnp.arange(columns, dtype=jnp.int32)[None, :]).astype(jnp.int32)
    position = jnp.sum((jnp.cumsum(named, axis=0) - named) * named, axis=1)
    destination = flat * capacity + position
    places = jnp.arange(columns * capacity, dtype=jnp.int32)
    choose = (places[:, None] == destination[None, :]).astype(jnp.bfloat16)
    by_slot = destination.reshape(tokens, top)
    token_of = sum(
        (places[:, None] == by_slot[None, :, slot]).astype(jnp.bfloat16) for slot in range(top)
    )
    scaled = (
        (gates[:, :, None] * hidden.astype(jnp.float32)).astype(jnp.bfloat16).reshape(slots, width)
    )
    packed = jnp.concatenate(
        [jnp.dot(choose, scaled, preferred_element_type=jnp.float32).astype(jnp.bfloat16), token_of], axis=1
    ).reshape(columns, capacity, width + tokens)

    sems = pltpu.SemaphoreType.DMA
    depth = columns // 2
    every, rows = pl.pallas_call(
        functools.partial(exchange, groups, columns),
        out_shape=(
            jax.ShapeDtypeStruct((columns, groups, tokens, part), jnp.bfloat16),
            jax.ShapeDtypeStruct((columns, groups, capacity, width + tokens), jnp.bfloat16),
        ),
        in_specs=[pl.BlockSpec(memory_space=pl.ANY)] * 2,
        out_specs=[pl.BlockSpec(memory_space=pl.ANY)] * 2,
        scratch_shapes=[
            sems((2,)),
            sems((groups,)),
            sems((groups,)),
            sems((depth, groups)),
            sems((depth, groups)),
            sems((depth, groups)),
            sems((depth, groups)),
            sems((depth, groups)),
            sems((columns,)),
            sems((columns,)),
            sems((groups, columns)),
            sems((groups, columns)),
        ],
        compiler_params=pltpu.CompilerParams(collective_id=0, has_side_effects=True),
        name="exchange",
    )(cotangent, packed)

    grad_matrix, returned = pl.pallas_call(
        functools.partial(product, groups, columns),
        out_shape=(
            jax.ShapeDtypeStruct((width, part), jnp.bfloat16),
            jax.ShapeDtypeStruct((columns, capacity, width), jnp.bfloat16),
        ),
        in_specs=[pl.BlockSpec(memory_space=pl.ANY)] + [pl.BlockSpec(memory_space=pltpu.VMEM)] * 2,
        out_specs=[pl.BlockSpec(memory_space=pltpu.VMEM)] * 2,
        scratch_shapes=[
            pltpu.VMEM((columns, groups, capacity, part), jnp.bfloat16),
            pltpu.VMEM((width, columns * groups * capacity), jnp.bfloat16),
            pltpu.VMEM((2, groups, tokens, part), jnp.bfloat16),
            pltpu.VMEM((columns, groups, capacity, width), jnp.bfloat16),
            pltpu.VMEM((groups, columns, capacity, width), jnp.bfloat16),
            pltpu.VMEM((columns, capacity, width), jnp.bfloat16),
            sems((groups, columns)),
            sems((groups, columns)),
            sems((columns,)),
            sems((columns,)),
            sems((2,)),
        ],
        compiler_params=pltpu.CompilerParams(
            collective_id=1, has_side_effects=True, vmem_limit_bytes=56 << 20
        ),
        name="product",
    )(every, weight[0], rows)
    back = lax.dot_general(
        choose, returned.reshape(columns * capacity, width), (((0,), (0,)), ((), ())), preferred_element_type=jnp.float32
    )
    grad_hidden = (
        (gates.reshape(slots)[:, None] * back).astype(jnp.bfloat16).reshape(tokens, top, width)
    )
    grad_gates = jnp.sum(
        hidden.reshape(slots, width).astype(jnp.float32) * back, axis=1
    ).reshape(tokens, top)
    return (grad_hidden, grad_gates, grad_matrix[None])


def dispatched(hidden, routes, gates, cotangent, weight):
    local_tokens, top_count, hidden_width = hidden.shape
    columns = lax.axis_size("expert")
    capacity = min(local_tokens, 2 * local_tokens * top_count // columns)
    slot_count = local_tokens * top_count
    flat_experts = routes.reshape(slot_count)
    one_hot = (flat_experts[:, None] == jnp.arange(columns, dtype=jnp.int32)[None, :]).astype(
        jnp.int32
    )
    earlier = jnp.cumsum(one_hot, axis=0) - one_hot
    position = jnp.sum(earlier * one_hot, axis=1)
    destination = flat_experts * capacity + position
    slot_of = (
        jnp.full((columns * capacity,), slot_count, jnp.int32)
        .at[destination]
        .set(jnp.arange(slot_count, dtype=jnp.int32))
    )
    scaled = (
        (gates[:, :, None] * hidden.astype(jnp.float32))
        .astype(jnp.bfloat16)
        .reshape(slot_count, hidden_width)
    )
    scaled = jnp.concatenate([scaled, jnp.zeros((1, hidden_width), jnp.bfloat16)], axis=0)
    cot_pad = jnp.concatenate([cotangent, jnp.zeros((1, cotangent.shape[1]), jnp.bfloat16)], axis=0)
    send_rows = scaled[slot_of].reshape(columns, capacity, hidden_width)
    send_cot = cot_pad[slot_of // top_count].reshape(columns, capacity, cotangent.shape[1])
    got_rows, got_cot = (
        lax.all_to_all(send_rows, "expert", split_axis=0, concat_axis=0, tiled=True),
        lax.all_to_all(send_cot, "expert", split_axis=0, concat_axis=0, tiled=True),
    )
    cot_quarter = lax.all_to_all(got_cot[None], "dp", split_axis=3, concat_axis=0, tiled=True)
    rows_all = lax.all_gather(got_rows[None], "dp", axis=0, tiled=True)
    matrix = weight[0]
    partial_back = jnp.einsum(
        "bscd,fd->bscf", cot_quarter, matrix, preferred_element_type=jnp.float32
    )
    summed = lax.psum_scatter(partial_back, "dp", scatter_dimension=0, tiled=True)
    grad_matrix = jnp.einsum(
        "bscf,bscd->fd", rows_all, cot_quarter, preferred_element_type=jnp.float32
    )
    returned = lax.all_to_all(summed[0], "expert", split_axis=0, concat_axis=0, tiled=True)
    back = returned.reshape(columns * capacity, hidden_width)[destination]
    grad_hidden = (
        (gates.reshape(slot_count)[:, None] * back)
        .astype(jnp.bfloat16)
        .reshape(local_tokens, top_count, hidden_width)
    )
    grad_gates = jnp.sum(
        hidden.reshape(slot_count, hidden_width).astype(jnp.float32) * back, axis=1
    ).reshape(local_tokens, top_count)
    return (grad_hidden, grad_gates, grad_matrix.astype(jnp.bfloat16)[None])


def per_device(hidden, routes, gates, cotangent, weight):
    tokens, top = routes.shape
    capacity = min(tokens, 2 * tokens * top // lax.axis_size("expert"))
    form = gathered if tokens <= 2 * capacity else dispatched
    return form(hidden, routes, gates, cotangent, weight)


def solution(mesh):
    placed = (
        P(("dp", "expert"), None, None),
        P(("dp", "expert"), None),
        P(("dp", "expert"), None),
        P(("dp", "expert"), None),
        P("expert", None, "dp"),
    )
    return jax.shard_map(
        per_device,
        mesh=mesh,
        in_specs=placed,
        out_specs=(
            P(("dp", "expert"), None, None),
            P(("dp", "expert"), None),
            P("expert", None, "dp"),
        ),
        check_vma=False,
    )
```
